32 devices in a mesh: group: 2 (over y), aper: 4 (over z), strip: 2 (over x), beam: 2 (over core).
Axes of the slice: x: 2, y: 2, z: 4, core: 2. Of those that a mesh axis runs over, the one named last changes fastest.
Arguments:
- partial_pictures: bfloat16 [2, 8, 128, 2048], P(None, ('group', 'aper'), 'beam', 'strip'), parts along dimension 1, may hold values from -6 to 6
- floor_input_direction: int32 [4, 8, 2, 128], P(None, ('group', 'aper'), None, 'beam'), parts along dimension 1, may hold values from 0 to 126
- higher_neighbour_blend: float32 [4, 8, 2, 128], P(None, ('group', 'aper'), None, 'beam'), parts along dimension 1, may hold values from 0 to 1
- integer_distance_bins: int32 [4, 8, 2, 128], P(None, ('group', 'aper'), None, 'beam'), parts along dimension 1, may hold values from -64 to 64
- distance_offset_fraction: float32 [4, 8, 2, 128], P(None, ('group', 'aper'), None, 'beam'), parts along dimension 1, may hold values from -0.5 to 0.5
- modulation_rotation: float32 [4, 8, 2, 128], P(None, ('group', 'aper'), None, 'beam'), parts along dimension 1, may hold values from -3.140625 to 3.140625
Outputs:
- focused: bfloat16 [2, 8, 128, 2048], P(None, ('group', 'aper'), 'beam', 'strip'), parts along dimension 1
The draws below stay inside these ranges and needn't reach their ends.
There are 2 independent parts, one for each index of `group`. The reference program is written for one: setup_inputs(seed, part) draws one part's arguments, and reference() takes and returns one part's arrays. A program takes and returns all parts, laid end to end along the dimension named above; each array names one. Nothing has to cross between parts.
Inputs may be any that keep to these rules, and one draw needn't show every extreme that they name: `floor_input_direction`: a lower source beam below the last beam.
All inputs are finite; a program needn't handle non-finite values.
Results may differ from the reference program's by a relative error of at most 0.025.
Values may be sent and summed in bfloat16 or wider, within the bound.
A program may use at most 64 MiB of HBM per device.

```python
import math
import jax
import jax.numpy as jnp
import numpy as np
from jax import lax

STRIP = 1024
GUARD = 128
RADIX = 32
NUM_COMBINES = 4
NUM_SUBARRAYS = 4
NUM_LOOK_DIRS = 128
RANGE = 2048
N_APER = 4


def shift_signs(key):
    table_shape = (NUM_COMBINES, NUM_SUBARRAYS, 2, NUM_LOOK_DIRS)
    coins = jax.random.randint(jax.random.fold_in(key, 4099), table_shape, 0, 2, dtype=jnp.int32)
    flat_values = (2 * coins - 1).reshape(-1)
    flat_values = flat_values.at[0].set(1).at[1].set(-1)
    return flat_values.reshape(table_shape)


def draw_integer_distance_bins(key, part):
    sign_table = shift_signs(key)
    table_shape = sign_table.shape
    half_guard = GUARD // 2
    first_key, second_key = jax.random.split(jax.random.fold_in(key, 811))
    chooser = jax.random.randint(first_key, table_shape, 0, 4, dtype=jnp.int32)
    spread_bins = jax.random.randint(second_key, table_shape, 0, half_guard + 1, dtype=jnp.int32)
    magnitude = jnp.where(chooser < 3, half_guard, spread_bins).astype(jnp.int32).reshape(-1)
    magnitude = magnitude.at[0].set(half_guard).at[1].set(half_guard)
    return (sign_table * magnitude.reshape(table_shape)).astype(jnp.int32)


def draw_distance_offset_fraction(key, part):
    sign_table = shift_signs(key).astype(jnp.float32)
    fraction_key = jax.random.fold_in(key, 977)
    magnitude = jax.random.uniform(fraction_key, sign_table.shape, jnp.float32, 0.3, 0.5)
    return sign_table * magnitude


def draw_partial_pictures(key, part):
    table_shape = (2, NUM_SUBARRAYS, NUM_LOOK_DIRS, RANGE)
    key_list = jax.random.split(key, 3)
    steps_index = jnp.arange(RANGE, dtype=jnp.int32)
    abscissa_grid = steps_index.astype(jnp.float32)
    broad_trend = 0.7 * jnp.clip(jax.random.normal(key_list[0], table_shape, jnp.float32), -3.0, 3.0)
    tone_gain = 1.6
    term_shape = (2, NUM_SUBARRAYS, NUM_LOOK_DIRS, 1)
    trace_outline = jnp.zeros(table_shape, jnp.float32)
    for term_index in range(8):
        term_key = jax.random.fold_in(key_list[1], term_index)
        freq_key, phase_key, weight_key = jax.random.split(term_key, 3)
        frequency = jax.random.uniform(freq_key, term_shape, jnp.float32, 0.0, 1.0 / (4.0 * GUARD))
        phase_value = jax.random.uniform(phase_key, term_shape, jnp.float32, -math.pi, math.pi)
        amplitude = jax.random.uniform(weight_key, term_shape, jnp.float32, -1.0, 1.0)
        trace_outline = trace_outline + amplitude * jnp.cos(2.0 * math.pi * frequency * abscissa_grid + phase_value)
    trace_outline = trace_outline * 0.87
    drift_speed = jax.random.uniform(key_list[2], (NUM_SUBARRAYS, NUM_LOOK_DIRS, 1), jnp.float32, 0.0, math.pi / (4.0 * GUARD))
    flipping_parity = (1 - 2 * (steps_index % 2)).astype(jnp.float32)
    tone_inphase = flipping_parity * jnp.cos(drift_speed * abscissa_grid)
    tone_quadrature = -flipping_parity * jnp.sin(drift_speed * abscissa_grid)
    keyed_trace_inphase = trace_outline[0] * tone_inphase - trace_outline[1] * tone_quadrature
    keyed_trace_quadrature = trace_outline[0] * tone_quadrature + trace_outline[1] * tone_inphase
    keyed_trace = jnp.stack([keyed_trace_inphase, keyed_trace_quadrature])
    boundary_gap = steps_index % STRIP
    boundary_gap = jnp.minimum(boundary_gap, STRIP - boundary_gap).astype(jnp.float32) / GUARD
    edge_boost = 1.0 + 0.8 * jnp.exp(-(boundary_gap * boundary_gap))
    end_gap = jnp.minimum(steps_index, RANGE - 1 - steps_index).astype(jnp.float32)
    fringe_decay = jnp.minimum(1.0, (end_gap + 0.5) / (2.0 * GUARD))
    picture_batch = edge_boost * (broad_trend + tone_gain * fringe_decay * keyed_trace)
    return jnp.clip(picture_batch, -6.0, 6.0).astype(jnp.bfloat16)


def with_ends(values, own_key, least, largest):
    place = [jax.random.randint(jax.random.fold_in(own_key, axis), (), 0, length) for axis, length in enumerate(values.shape)]
    widest = values.shape.index(max(values.shape))
    next_to = place[:widest] + [(place[widest] + 1) % values.shape[widest]] + place[widest + 1:]
    return values.at[tuple(place)].set(least).at[tuple(next_to)].set(largest)


def block_scale(rng, shape, cuts, least, high):
    gain, own = 1.0, jax.random.fold_in(rng, 6)
    for axis_at, shards_of in cuts:
        steps = jnp.exp(jax.random.uniform(jax.random.fold_in(own, axis_at), (shards_of,), jnp.float32, least / len(cuts), high / len(cuts)))
        gain = gain * jnp.repeat(steps, shape[axis_at] // shards_of).reshape([-1 if axis == axis_at else 1 for axis in range(len(shape))])
    return gain


def setup_inputs(seed: int = 0, part: int = 0) -> dict:
    streams_of = jax.random.split(jax.random.key(seed), 7)
    part_splits = jax.random.split(jax.random.fold_in(streams_of[6], part), 7)
    return {
        "partial_pictures": draw_partial_pictures(jax.random.fold_in(jax.random.fold_in(streams_of[6], part), 71), part),
        "floor_input_direction": with_ends(jax.random.randint(part_splits[1], (NUM_COMBINES, NUM_SUBARRAYS, 2, NUM_LOOK_DIRS), 0, NUM_LOOK_DIRS - 1), jax.random.fold_in(part_splits[1], 1), 0, (NUM_LOOK_DIRS - 1) - 1).astype(jnp.int32),
        "higher_neighbour_blend": jnp.clip(1.0 * jax.random.uniform(part_splits[2], (NUM_COMBINES, NUM_SUBARRAYS, 2, NUM_LOOK_DIRS), jnp.float32) ** block_scale(part_splits[2], (NUM_COMBINES, NUM_SUBARRAYS, 2, NUM_LOOK_DIRS), ((1, 4), (3, 2)), -0.2, 0.2), 0.0, 1.0),
        "integer_distance_bins": draw_integer_distance_bins(jax.random.fold_in(jax.random.fold_in(streams_of[6], part), 71), part),
        "distance_offset_fraction": draw_distance_offset_fraction(jax.random.fold_in(jax.random.fold_in(streams_of[6], part), 71), part),
        "modulation_rotation": jnp.clip(jax.random.uniform(part_splits[5], (NUM_COMBINES, NUM_SUBARRAYS, 2, NUM_LOOK_DIRS), jnp.float32, -3.140625, 3.140625), -3.140625, 3.140625),
    }


def square_tables(size):
    indices = jnp.arange(size, dtype=jnp.int32)
    product = (indices[:, None] * indices[None, :]) % size
    angle = product.astype(jnp.float32) * (2.0 * math.pi / size)
    return jnp.cos(angle).astype(jnp.bfloat16), jnp.sin(angle).astype(jnp.bfloat16)


def spectral_tables(length, radix):
    columns = length // radix
    first_cos, first_sin = square_tables(radix)
    second_cos, second_sin = square_tables(columns)
    lead = jnp.arange(radix, dtype=jnp.int32)
    trail = jnp.arange(columns, dtype=jnp.int32)
    angle = ((lead[:, None] * trail[None, :]) % length).astype(jnp.float32) * (2.0 * math.pi / length)
    return (first_cos, first_sin, second_cos, second_sin, jnp.cos(angle), jnp.sin(angle))


def over_first(values, table):
    return jnp.einsum('rab,ak->rkb', values.astype(jnp.float32), table.astype(jnp.float32), precision=lax.Precision.HIGHEST)


def over_last(values, table):
    return jnp.einsum('rkb,bm->rkm', values.astype(jnp.float32), table.astype(jnp.float32), precision=lax.Precision.HIGHEST)


def forward_ramp(window, shift_whole, shift_part, rotation_radians, tables, radix):
    first_cos, first_sin, second_cos, second_sin, twist_cos, twist_sin = tables
    length = window.shape[-1]
    rows = window.shape[1]
    columns = length // radix
    real_part = window[0].reshape(rows, radix, columns)
    imag_part = window[1].reshape(rows, radix, columns)
    section_real = over_first(real_part, first_cos) + over_first(imag_part, first_sin)
    section_imag = over_first(imag_part, first_cos) - over_first(real_part, first_sin)
    twisted_real = (section_real * twist_cos - (-section_imag) * twist_sin * 0.0 + section_imag * twist_sin).astype(jnp.bfloat16)
    twisted_imag = (section_imag * twist_cos - section_real * twist_sin).astype(jnp.bfloat16)
    spec_real = over_last(twisted_real, second_cos) + over_last(twisted_imag, second_sin)
    spec_imag = over_last(twisted_imag, second_cos) - over_last(twisted_real, second_sin)
    flat = jnp.arange(length, dtype=jnp.int32)
    freqs = flat // columns + radix * (flat % columns)
    signed = jnp.where(freqs < length // 2, freqs, freqs - length).astype(jnp.float32)
    sigma = shift_whole.astype(jnp.float32) + shift_part
    theta = rotation_radians[:, None] - (2.0 * math.pi / length) * signed[None, :] * sigma[:, None]
    theta = theta.reshape(rows, radix, columns)
    cos_theta = jnp.cos(theta)
    sin_theta = jnp.sin(theta)
    ramp_real = (spec_real * cos_theta - spec_imag * sin_theta).astype(jnp.bfloat16)
    ramp_imag = (spec_real * sin_theta + spec_imag * cos_theta).astype(jnp.bfloat16)
    return jnp.stack([ramp_real, ramp_imag])


def inverse_part(merged, tables, guard, strip):
    first_cos, first_sin, second_cos, second_sin, twist_cos, twist_sin = tables
    rows = merged.shape[1]
    length = merged.shape[2] * merged.shape[3]
    back_real = over_last(merged[0], second_cos) - over_last(merged[1], second_sin)
    back_imag = over_last(merged[1], second_cos) + over_last(merged[0], second_sin)
    untwisted_real = (back_real * twist_cos - back_imag * twist_sin).astype(jnp.bfloat16)
    untwisted_imag = (back_imag * twist_cos + back_real * twist_sin).astype(jnp.bfloat16)
    out_real = over_first(untwisted_real, first_cos) - over_first(untwisted_imag, first_sin)
    out_imag = over_first(untwisted_imag, first_cos) + over_first(untwisted_real, first_sin)
    out_real = out_real.reshape(rows, length)[:, guard:guard + strip] * (1.0 / length)
    out_imag = out_imag.reshape(rows, length)[:, guard:guard + strip] * (1.0 / length)
    return jnp.stack([out_real, out_imag]).astype(jnp.bfloat16)


def reference(partial_pictures, floor_input_direction, higher_neighbour_blend, integer_distance_bins, distance_offset_fraction, modulation_rotation):
    apers = partial_pictures.shape[1]
    beams = partial_pictures.shape[2]
    extent = partial_pictures.shape[3]
    strips = extent // STRIP
    length = STRIP + 2 * GUARD
    tables = spectral_tables(length, RADIX)
    partner_bits = N_APER.bit_length() - 1
    columns = jnp.arange(beams, dtype=jnp.int32)
    zero_value = jnp.zeros((), jnp.bfloat16)
    current = partial_pictures
    for combine_depth in range(NUM_COMBINES):
        padded = jnp.pad(current, ((0, 0), (0, 0), (0, 0), (GUARD, GUARD)))
        windows = jnp.stack([padded[:, :, :, strip_index * STRIP:strip_index * STRIP + length] for strip_index in range(strips)], axis=3)
        partner = np.arange(apers) ^ (1 << (combine_depth % partner_bits))
        terms = []
        for direction_position in range(2):
            source = windows if direction_position == 0 else windows[:, partner]
            chosen = floor_input_direction[combine_depth, :, direction_position, :][:, :, None]
            fraction = higher_neighbour_blend[combine_depth, :, direction_position, :]
            lower = (1.0 - fraction).astype(jnp.bfloat16)[:, :, None]
            upper = fraction.astype(jnp.bfloat16)[:, :, None]
            weights = jnp.where(columns == chosen, lower, zero_value) + jnp.where(columns == chosen + 1, upper, zero_value)
            interp = jnp.einsum('abj,cajnw->cabnw', weights.astype(jnp.float32), source.astype(jnp.float32), precision=lax.Precision.HIGHEST).astype(jnp.bfloat16)
            flat_rows = interp.reshape(2, apers * beams * strips, length)
            matrix_arrangement = (apers, beams, strips)
            whole_bins = jnp.broadcast_to(integer_distance_bins[combine_depth, :, direction_position, :][:, :, None], matrix_arrangement).reshape(-1)
            part_bins = jnp.broadcast_to(distance_offset_fraction[combine_depth, :, direction_position, :][:, :, None], matrix_arrangement).reshape(-1)
            rotation_radians = jnp.broadcast_to(modulation_rotation[combine_depth, :, direction_position, :][:, :, None], matrix_arrangement).reshape(-1)
            terms.append(forward_ramp(flat_rows, whole_bins, part_bins, rotation_radians, tables, RADIX))
        merged = (terms[0].astype(jnp.float32) + terms[1].astype(jnp.float32)).astype(jnp.bfloat16)
        shifted = inverse_part(merged, tables, GUARD, STRIP)
        current = shifted.reshape(2, apers, beams, strips, STRIP).reshape(2, apers, beams, extent)
    return current
```

```python
import functools
import math

import jax
import jax.numpy as jnp
import ml_dtypes
import numpy as np
from jax import lax
from jax.experimental import pallas as pl
from jax.experimental.pallas import tpu as pltpu
from jax.sharding import PartitionSpec as P

GUARD = 128
NUM_COMBINES = 4
CHUNK = 256
LANES = 128
MESH = pl.DeviceIdType.MESH
F32 = jnp.float32
BF16 = jnp.bfloat16


def transform_tables(strip_len):
    length = strip_len + 2 * GUARD
    half = length // 2
    sample = np.concatenate(
        [np.arange(GUARD, GUARD + strip_len), np.arange(GUARD), np.arange(GUARD + strip_len, length)]
    )
    freq = np.arange(half)
    angle = (sample[:, None] * freq[None, :] % length) * (2.0 * np.pi / length)
    cosines = np.cos(angle)
    sines = np.sin(angle)
    sines[:, 0] = 1.0 - 2.0 * (sample % 2)
    forward = np.concatenate([cosines, sines], axis=1).astype(ml_dtypes.bfloat16)
    inverse = forward[:strip_len].astype(np.float32).T.copy()
    inverse[0] *= 0.5
    inverse[half] *= 0.5
    return forward, inverse.astype(ml_dtypes.bfloat16)


def kernel(
    n_aper,
    n_strip,
    x_ref,
    floor_ref,
    blend_ref,
    bins_ref,
    part_ref,
    rot_ref,
    fwd_hbm,
    inv_hbm,
    out_ref,
    fwd,
    inv,
    full,
    guard,
    w_own,
    w_send,
    w_recv,
    s_main,
    s_guard,
    r_main,
    r_guard,
    x_own,
    acc,
    merged,
    cos_t,
    sin_t,
    table_sem,
    core_send,
    core_recv,
    edge_send,
    edge_recv,
    z_send,
    z_recv,
    w_send_sem,
    w_recv_sem,
):
    beams = x_ref.shape[1]
    all_beams = 2 * beams
    strip_len = x_ref.shape[2]
    chunks = strip_len // CHUNK
    length = strip_len + 2 * GUARD
    half = length // 2
    blocks = half // LANES
    bits = n_aper.bit_length() - 1
    order = [0, chunks - 1] + list(range(1, chunks - 1))

    aper = lax.axis_index("aper")
    strip = lax.axis_index("strip")
    beam = lax.axis_index("beam")
    other = 1 - beam
    has_left = strip > 0
    has_right = strip < n_strip - 1
    mine = pl.ds(pl.multiple_of(beam * beams, beams), beams)

    table_copies = [
        pltpu.make_async_copy(fwd_hbm, fwd, table_sem.at[0]),
        pltpu.make_async_copy(inv_hbm, inv, table_sem.at[1]),
    ]
    for copy in table_copies:
        copy.start()

    def flip(bit):
        return aper + bit - 2 * bit * ((aper // bit) % 2)

    def level_bit(level):
        bit = 1 << ((NUM_COMBINES - 1) % bits)
        for at in range(NUM_COMBINES - 1):
            bit = jnp.where(level == at, 1 << (at % bits), bit)
        return bit

    barrier = pltpu.get_barrier_semaphore()

    def greet(where):
        pl.semaphore_signal(barrier, inc=1, device_id=where, device_id_type=MESH)

    greet({"beam": other})
    partner_bits = sorted({1 << (at % bits) for at in range(NUM_COMBINES)})
    for bit in partner_bits:
        greet({"aper": flip(bit)})

    @pl.when(has_left)
    def _():
        greet({"strip": strip - 1})
        greet({"strip": strip - 1, "beam": other})

    @pl.when(has_right)
    def _():
        greet({"strip": strip + 1})
        greet({"strip": strip + 1, "beam": other})

    sides = has_left.astype(jnp.int32) + has_right.astype(jnp.int32)
    pl.semaphore_wait(barrier, 1 + len(partner_bits) + 2 * sides)

    def core_copy(level, j):
        place = full.at[level, j, :, mine, :]
        return pltpu.make_async_remote_copy(
            place, place, core_send.at[level, j], core_recv.at[level, j], {"beam": other}, MESH
        )

    def edge_copy(level, side, cross):
        j, at = (chunks - 1, CHUNK - GUARD) if side == 0 else (0, 0)
        target = strip + 1 if side == 0 else strip - 1
        return pltpu.make_async_remote_copy(
            full.at[level, j, :, mine, pl.ds(at, GUARD)],
            guard.at[level, side, :, mine, :],
            edge_send.at[level, side, cross],
            edge_recv.at[level, side, cross],
            {"strip": target, "beam": other if cross else beam},
            MESH,
        )

    def edge_wait(level, side, cross):
        place = guard.at[level, side, :, mine, :]
        pltpu.make_async_remote_copy(
            place, place, edge_send.at[level, side, cross], edge_recv.at[level, side, cross], {"beam": other}, MESH
        ).wait_recv()

    def z_copy(level, j):
        return pltpu.make_async_remote_copy(
            s_main.at[level, j],
            r_main.at[level, j],
            z_send.at[level, j],
            z_recv.at[level, j],
            {"aper": flip(level_bit(level))},
            MESH,
        )

    def z_guard_copy(level, side):
        return pltpu.make_async_remote_copy(
            s_guard.at[level, side],
            r_guard.at[level, side],
            z_send.at[level, chunks + side],
            z_recv.at[level, chunks + side],
            {"aper": flip(level_bit(level))},
            MESH,
        )

    def w_copy(level):
        return pltpu.make_async_remote_copy(
            w_send.at[level],
            w_recv.at[level],
            w_send_sem.at[level],
            w_recv_sem.at[level],
            {"aper": flip(level_bit(level))},
            MESH,
        )

    def distribute(level, j):
        core_copy(level, j).start()
        if j == 0:

            @pl.when(has_left)
            def _():
                for cross in range(2):
                    edge_copy(level, 1, cross).start()

        if j == chunks - 1:

            @pl.when(has_right)
            def _():
                for cross in range(2):
                    edge_copy(level, 0, cross).start()

    for j in order:
        full[0, j, :, mine, :] = x_ref[:, :, j * CHUNK : (j + 1) * CHUNK]
        distribute(0, j)

    eye = lax.broadcasted_iota(jnp.int32, (beams, beams), 0) == lax.broadcasted_iota(
        jnp.int32, (beams, beams), 1
    )

    def column(ref, level, slot):
        row = ref[level, slot : slot + 1, :].astype(F32)
        return jnp.sum(jnp.where(eye, jnp.broadcast_to(row, (beams, beams)), 0.0), axis=1, keepdims=True)

    def weights_of(level, slot):
        source = lax.broadcasted_iota(jnp.int32, (beams, all_beams), 1).astype(F32)
        chosen = column(floor_ref, level, slot)
        fraction = column(blend_ref, level, slot)
        return (
            jnp.where(source == chosen, 1.0 - fraction, 0.0)
            + jnp.where(source == chosen + 1.0, fraction, 0.0)
        ).astype(BF16)

    def send_weights(level, carry):
        w_send[level] = weights_of(level, 1)
        w_copy(level).start()
        return carry

    lax.fori_loop(0, NUM_COMBINES, send_weights, 0)

    @pl.when(jnp.logical_not(has_left))
    def _():
        guard[:, 0] = jnp.zeros((NUM_COMBINES,) + guard.shape[2:], BF16)
        r_guard[:, 0] = jnp.zeros((NUM_COMBINES,) + r_guard.shape[2:], BF16)

    @pl.when(jnp.logical_not(has_right))
    def _():
        guard[:, 1] = jnp.zeros((NUM_COMBINES,) + guard.shape[2:], BF16)
        r_guard[:, 1] = jnp.zeros((NUM_COMBINES,) + r_guard.shape[2:], BF16)

    def own_weights(level, carry):
        w_own[level] = weights_of(level, 0)
        return carry

    lax.fori_loop(0, NUM_COMBINES, own_weights, 0)

    step = 2.0 * math.pi / length
    lane = lax.broadcasted_iota(jnp.int32, (beams, LANES), 1)

    def level_body(level, carry):
        w_copy(level).wait_recv()
        weights = jnp.concatenate([w_recv[level], w_own[level]], axis=0)
        for j in order:
            core_copy(level, j).wait_recv()
            for c in range(2):
                mixed = jnp.dot(weights, full[level, j, c], preferred_element_type=F32).astype(BF16)
                s_main[level, j, c * beams : (c + 1) * beams, :] = mixed[:beams]
                x_own[c * beams : (c + 1) * beams, j * CHUNK : (j + 1) * CHUNK] = mixed[beams:]
            z_copy(level, j).start()
        for side, there in ((0, has_left), (1, has_right)):

            @pl.when(there)
            def _():
                for cross in range(2):
                    edge_wait(level, side, cross)

            at = strip_len + side * GUARD
            for c in range(2):
                mixed = jnp.dot(weights, guard[level, side, c], preferred_element_type=F32).astype(BF16)
                s_guard[level, side, c * beams : (c + 1) * beams, :] = mixed[:beams]
                x_own[c * beams : (c + 1) * beams, at : at + GUARD] = mixed[beams:]

            @pl.when(there)
            def _():
                z_guard_copy(level, side).start()

        turns = []
        for slot in range(2):
            sigma = column(bins_ref, level, slot) + column(part_ref, level, slot)
            rot = column(rot_ref, level, slot)
            base = lane.astype(F32) * (step * sigma)
            base_cos, base_sin = jnp.cos(base), jnp.sin(base)
            lead = lane.astype(F32) * (step * LANES * sigma)
            lead_cos, lead_sin = jnp.cos(lead), jnp.sin(lead)
            for a in range(blocks):
                a_cos, a_sin = lead_cos[:, a : a + 1], lead_sin[:, a : a + 1]
                cos_t[slot, :, a * LANES : (a + 1) * LANES] = base_cos * a_cos - base_sin * a_sin
                sin_t[slot, :, a * LANES : (a + 1) * LANES] = base_sin * a_cos + base_cos * a_sin
            nyquist = rot + jnp.where(lane == 0, math.pi * sigma, 0.0)
            scale = 2.0 / length
            first = (jnp.cos(nyquist) * scale, jnp.sin(nyquist) * scale)
            rest = (first[0][:, 1:2], first[1][:, 1:2])
            turns.append((rest, first))

        @pl.when(level == 0)
        def _():
            table_copies[0].wait()

        for at in range(0, length, CHUNK):
            acc[0, :, at : at + CHUNK] = jnp.dot(x_own[...], fwd[:, at : at + CHUNK], preferred_element_type=F32)
        for i, j in enumerate(order + [chunks]):
            if j < chunks:
                z_copy(level, j).wait_recv()
                piece = r_main[level, j]
            else:
                for side, there in ((0, has_left), (1, has_right)):

                    @pl.when(there)
                    def _():
                        z_guard_copy(level, side).wait_recv()

                piece = jnp.concatenate([r_guard[level, 0], r_guard[level, 1]], axis=1)
            for at in range(0, length, CHUNK):
                term = jnp.dot(piece, fwd[j * CHUNK : (j + 1) * CHUNK, at : at + CHUNK], preferred_element_type=F32)
                if i == 0:
                    acc[1, :, at : at + CHUNK] = term
                else:
                    acc[1, :, at : at + CHUNK] += term

        for a in range(blocks):
            low = slice(a * LANES, (a + 1) * LANES)
            high = slice(half + a * LANES, half + (a + 1) * LANES)
            total = [0.0, 0.0, 0.0, 0.0]
            for slot in range(2):
                p_re, p_im = acc[slot, :beams, low], acc[slot, beams:, low]
                q_re, q_im = acc[slot, :beams, high], acc[slot, beams:, high]
                c, s = cos_t[slot, :, low], sin_t[slot, :, low]
                (rc, rs), first = turns[slot]
                qc, qs = first if a == 0 else (rc, rs)
                u_re, u_im = p_re * c - q_re * s, p_im * c - q_im * s
                v_re, v_im = q_re * c + p_re * s, q_im * c + p_im * s
                total[0] += u_re * rc - u_im * rs
                total[1] += u_im * rc + u_re * rs
                total[2] += v_re * qc - v_im * qs
                total[3] += v_im * qc + v_re * qs
            merged[:beams, low] = total[0].astype(BF16)
            merged[beams:, low] = total[1].astype(BF16)
            merged[:beams, high] = total[2].astype(BF16)
            merged[beams:, high] = total[3].astype(BF16)

        @pl.when(level == 0)
        def _():
            table_copies[1].wait()

        for j in order:
            cols = slice(j * CHUNK, (j + 1) * CHUNK)
            result = jnp.dot(merged[...], inv[:, cols], preferred_element_type=F32).astype(BF16)

            @pl.when(level < NUM_COMBINES - 1)
            def _():
                full[level + 1, j, 0, mine, :] = result[:beams]
                full[level + 1, j, 1, mine, :] = result[beams:]
                distribute(level + 1, j)

            @pl.when(level == NUM_COMBINES - 1)
            def _():
                out_ref[0, :, cols] = result[:beams]
                out_ref[1, :, cols] = result[beams:]

        return carry

    lax.fori_loop(0, NUM_COMBINES, level_body, 0)

    def drain(level, carry):
        w_copy(level).wait_send()
        for j in range(chunks):
            core_copy(level, j).wait_send()
            z_copy(level, j).wait_send()

        @pl.when(has_right)
        def _():
            for cross in range(2):
                edge_copy(level, 0, cross).wait_send()
            z_guard_copy(level, 1).wait_send()

        @pl.when(has_left)
        def _():
            for cross in range(2):
                edge_copy(level, 1, cross).wait_send()
            z_guard_copy(level, 0).wait_send()

        return carry

    lax.fori_loop(0, NUM_COMBINES, drain, 0)


def shards(pictures, floors, blends, bins, parts, rots):
    current = pictures[:, 0]
    _, beams, strip_len = current.shape
    length = strip_len + 2 * GUARD
    half = length // 2
    chunks = strip_len // CHUNK
    rows = 2 * beams
    forward, inverse = transform_tables(strip_len)
    n = NUM_COMBINES
    vmem = pl.BlockSpec(memory_space=pltpu.VMEM)
    dma = pltpu.SemaphoreType.DMA
    out = pl.pallas_call(
        functools.partial(kernel, lax.axis_size("aper"), lax.axis_size("strip")),
        out_shape=jax.ShapeDtypeStruct(current.shape, BF16),
        in_specs=[vmem] * 6 + [pl.BlockSpec(memory_space=pl.ANY)] * 2,
        out_specs=vmem,
        scratch_shapes=[
            pltpu.VMEM((length, length), BF16),
            pltpu.VMEM((length, strip_len), BF16),
            pltpu.VMEM((n, chunks, 2, 2 * beams, CHUNK), BF16),
            pltpu.VMEM((n, 2, 2, 2 * beams, GUARD), BF16),
            pltpu.VMEM((n, beams, 2 * beams), BF16),
            pltpu.VMEM((n, beams, 2 * beams), BF16),
            pltpu.VMEM((n, beams, 2 * beams), BF16),
            pltpu.VMEM((n, chunks, rows, CHUNK), BF16),
            pltpu.VMEM((n, 2, rows, GUARD), BF16),
            pltpu.VMEM((n, chunks, rows, CHUNK), BF16),
            pltpu.VMEM((n, 2, rows, GUARD), BF16),
            pltpu.VMEM((rows, length), BF16),
            pltpu.VMEM((2, rows, length), F32),
            pltpu.VMEM((rows, length), BF16),
            pltpu.VMEM((2, beams, half), F32),
            pltpu.VMEM((2, beams, half), F32),
            dma((2,)),
            dma((n, chunks)),
            dma((n, chunks)),
            dma((n, 2, 2)),
            dma((n, 2, 2)),
            dma((n, chunks + 2)),
            dma((n, chunks + 2)),
            dma((n,)),
            dma((n,)),
        ],
        compiler_params=pltpu.CompilerParams(
            collective_id=0, has_side_effects=True, vmem_limit_bytes=56 * 1024 * 1024
        ),
    )(
        current,
        floors[:, 0],
        blends[:, 0],
        bins[:, 0],
        parts[:, 0],
        rots[:, 0],
        jnp.asarray(forward),
        jnp.asarray(inverse),
    )
    return out[:, None]


def solution(mesh):
    tables = P(None, ("group", "aper"), None, "beam")
    pictures = P(None, ("group", "aper"), "beam", "strip")
    return jax.shard_map(
        shards,
        mesh=mesh,
        in_specs=(pictures,) + (tables,) * 5,
        out_specs=pictures,
        check_vma=False,
    )
```

```python
import functools
import math

import jax
import jax.numpy as jnp
import ml_dtypes
import numpy as np
from jax import lax
from jax.experimental import pallas as pl
from jax.experimental.pallas import tpu as pltpu
from jax.sharding import PartitionSpec as P

GUARD = 128
NUM_COMBINES = 4
CHUNK = 256
LANES = 128
MESH = pl.DeviceIdType.MESH
F32 = jnp.float32
BF16 = jnp.bfloat16


def transform_tables(strip_len):
    length = strip_len + 2 * GUARD
    half = length // 2
    sample = np.concatenate(
        [np.arange(GUARD, GUARD + strip_len), np.arange(GUARD), np.arange(GUARD + strip_len, length)]
    )
    freq = np.arange(half)
    angle = (sample[:, None] * freq[None, :] % length) * (2.0 * np.pi / length)
    cosines = np.cos(angle)
    sines = np.sin(angle)
    sines[:, 0] = 1.0 - 2.0 * (sample % 2)
    forward = np.concatenate([cosines, sines], axis=1).astype(ml_dtypes.bfloat16)
    inverse = forward[:strip_len].astype(np.float32).T.copy()
    inverse[0] *= 0.5
    inverse[half] *= 0.5
    return forward, inverse.astype(ml_dtypes.bfloat16)


def kernel(
    n_aper,
    n_strip,
    x_ref,
    floor_ref,
    blend_ref,
    bins_ref,
    part_ref,
    rot_ref,
    fwd_hbm,
    inv_hbm,
    out_ref,
    fwd,
    inv,
    full,
    w_own,
    w_send,
    w_recv,
    s_main,
    r_main,
    r_guard,
    x_own,
    acc,
    merged,
    cos_t,
    sin_t,
    table_sem,
    core_send,
    core_recv,
    edge_send,
    edge_recv,
    z_send,
    z_recv,
    w_send_sem,
    w_recv_sem,
):
    beams = x_ref.shape[1]
    all_beams = 2 * beams
    strip_len = x_ref.shape[2]
    chunks = strip_len // CHUNK
    length = strip_len + 2 * GUARD
    half = length // 2
    blocks = half // LANES
    bits = n_aper.bit_length() - 1
    order = [0, chunks - 1] + list(range(1, chunks - 1))

    aper = lax.axis_index("aper")
    strip = lax.axis_index("strip")
    beam = lax.axis_index("beam")
    other = 1 - beam
    has_left = strip > 0
    has_right = strip < n_strip - 1
    mine = pl.ds(pl.multiple_of(beam * beams, beams), beams)

    table_copies = [
        pltpu.make_async_copy(fwd_hbm, fwd, table_sem.at[0]),
        pltpu.make_async_copy(inv_hbm, inv, table_sem.at[1]),
    ]
    for copy in table_copies:
        copy.start()

    def flip(bit):
        return aper + bit - 2 * bit * ((aper // bit) % 2)

    def level_bit(level):
        bit = 1 << ((NUM_COMBINES - 1) % bits)
        for at in range(NUM_COMBINES - 1):
            bit = jnp.where(level == at, 1 << (at % bits), bit)
        return bit

    barrier = pltpu.get_barrier_semaphore()

    def greet(where):
        pl.semaphore_signal(barrier, inc=1, device_id=where, device_id_type=MESH)

    greet({"beam": other})
    partner_bits = sorted({1 << (at % bits) for at in range(NUM_COMBINES)})
    for bit in partner_bits:
        greet({"aper": flip(bit)})

    @pl.when(has_left)
    def _():
        greet({"strip": strip - 1})

    @pl.when(has_right)
    def _():
        greet({"strip": strip + 1})

    sides = has_left.astype(jnp.int32) + has_right.astype(jnp.int32)
    pl.semaphore_wait(barrier, 1 + len(partner_bits) + sides)

    def core_copy(level, j):
        place = full.at[level, j, :, mine, :]
        return pltpu.make_async_remote_copy(
            place, place, core_send.at[level, j], core_recv.at[level, j], {"beam": other}, MESH
        )

    def edge_copy(level, slot, side, outward=True):
        target = strip + 1 if (side == 0) == outward else strip - 1
        if slot == 0:
            at = strip_len - GUARD if side == 0 else 0
            source = x_own.at[level, :, pl.ds(at, GUARD)]
            place = x_own.at[level, :, pl.ds(strip_len + side * GUARD, GUARD)]
        else:
            j, at = (chunks - 1, CHUNK - GUARD) if side == 0 else (0, 0)
            source = r_main.at[level, j, :, pl.ds(at, GUARD)]
            place = r_guard.at[level, :, pl.ds(side * GUARD, GUARD)]
        return pltpu.make_async_remote_copy(
            source,
            place,
            edge_send.at[level, slot, side],
            edge_recv.at[level, slot, side],
            {"strip": target},
            MESH,
        )

    def send_edges(level, slot, j):
        if j == 0:

            @pl.when(has_left)
            def _():
                edge_copy(level, slot, 1).start()

        if j == chunks - 1:

            @pl.when(has_right)
            def _():
                edge_copy(level, slot, 0).start()

    def await_edges(level, slot):
        for side, there in ((0, has_left), (1, has_right)):

            @pl.when(there)
            def _():
                edge_copy(level, slot, side, outward=False).wait_recv()

    def z_copy(level, j):
        return pltpu.make_async_remote_copy(
            s_main.at[level, j],
            r_main.at[level, j],
            z_send.at[level, j],
            z_recv.at[level, j],
            {"aper": flip(level_bit(level))},
            MESH,
        )

    def w_copy(level):
        return pltpu.make_async_remote_copy(
            w_send.at[level],
            w_recv.at[level],
            w_send_sem.at[level],
            w_recv_sem.at[level],
            {"aper": flip(level_bit(level))},
            MESH,
        )

    def distribute(level, j):
        core_copy(level, j).start()

    for j in order:
        full[0, j, :, mine, :] = x_ref[:, :, j * CHUNK : (j + 1) * CHUNK]
        distribute(0, j)

    eye = lax.broadcasted_iota(jnp.int32, (beams, beams), 0) == lax.broadcasted_iota(
        jnp.int32, (beams, beams), 1
    )

    def column(ref, level, slot):
        row = ref[level, slot : slot + 1, :].astype(F32)
        return jnp.sum(jnp.where(eye, jnp.broadcast_to(row, (beams, beams)), 0.0), axis=1, keepdims=True)

    def weights_of(level, slot):
        source = lax.broadcasted_iota(jnp.int32, (beams, all_beams), 1).astype(F32)
        chosen = column(floor_ref, level, slot)
        fraction = column(blend_ref, level, slot)
        return (
            jnp.where(source == chosen, 1.0 - fraction, 0.0)
            + jnp.where(source == chosen + 1.0, fraction, 0.0)
        ).astype(BF16)

    def send_weights(level, carry):
        w_send[level] = weights_of(level, 1)
        w_copy(level).start()
        return carry

    lax.fori_loop(0, NUM_COMBINES, send_weights, 0)

    @pl.when(jnp.logical_not(has_left))
    def _():
        none = jnp.zeros((NUM_COMBINES, 2 * beams, GUARD), BF16)
        x_own[:, :, strip_len + 0 * GUARD : strip_len + 1 * GUARD] = none
        r_guard[:, :, 0 * GUARD : 1 * GUARD] = none

    @pl.when(jnp.logical_not(has_right))
    def _():
        none = jnp.zeros((NUM_COMBINES, 2 * beams, GUARD), BF16)
        x_own[:, :, strip_len + 1 * GUARD : strip_len + 2 * GUARD] = none
        r_guard[:, :, 1 * GUARD : 2 * GUARD] = none

    def own_weights(level, carry):
        w_own[level] = weights_of(level, 0)
        return carry

    lax.fori_loop(0, NUM_COMBINES, own_weights, 0)

    step = 2.0 * math.pi / length
    lane = lax.broadcasted_iota(jnp.int32, (beams, LANES), 1)

    def level_body(level, carry):
        w_copy(level).wait_recv()
        weights = jnp.concatenate([w_recv[level], w_own[level]], axis=0)
        for j in order:
            core_copy(level, j).wait_recv()
            for c in range(2):
                mixed = jnp.dot(weights, full[level, j, c], preferred_element_type=F32).astype(BF16)
                s_main[level, j, c * beams : (c + 1) * beams, :] = mixed[:beams]
                x_own[level, c * beams : (c + 1) * beams, j * CHUNK : (j + 1) * CHUNK] = mixed[beams:]
            z_copy(level, j).start()
            send_edges(level, 0, j)
        turns = []
        for slot in range(2):
            sigma = column(bins_ref, level, slot) + column(part_ref, level, slot)
            rot = column(rot_ref, level, slot)
            base = lane.astype(F32) * (step * sigma)
            base_cos, base_sin = jnp.cos(base), jnp.sin(base)
            lead = lane.astype(F32) * (step * LANES * sigma)
            lead_cos, lead_sin = jnp.cos(lead), jnp.sin(lead)
            for a in range(blocks):
                a_cos, a_sin = lead_cos[:, a : a + 1], lead_sin[:, a : a + 1]
                cos_t[slot, :, a * LANES : (a + 1) * LANES] = base_cos * a_cos - base_sin * a_sin
                sin_t[slot, :, a * LANES : (a + 1) * LANES] = base_sin * a_cos + base_cos * a_sin
            nyquist = rot + jnp.where(lane == 0, math.pi * sigma, 0.0)
            scale = 2.0 / length
            first = (jnp.cos(nyquist) * scale, jnp.sin(nyquist) * scale)
            rest = (first[0][:, 1:2], first[1][:, 1:2])
            turns.append((rest, first))

        @pl.when(level == 0)
        def _():
            table_copies[0].wait()

        await_edges(level, 0)
        for at in range(0, length, CHUNK):
            acc[0, :, at : at + CHUNK] = jnp.dot(x_own[level], fwd[:, at : at + CHUNK], preferred_element_type=F32)
        for i, j in enumerate(order[:-1] + [chunks, order[-1]]):
            if j < chunks:
                z_copy(level, j).wait_recv()
                send_edges(level, 1, j)
                piece = r_main[level, j]
            else:
                await_edges(level, 1)
                piece = r_guard[level]
            for at in range(0, length, CHUNK):
                term = jnp.dot(piece, fwd[j * CHUNK : (j + 1) * CHUNK, at : at + CHUNK], preferred_element_type=F32)
                if i == 0:
                    acc[1, :, at : at + CHUNK] = term
                else:
                    acc[1, :, at : at + CHUNK] += term

        for a in range(blocks):
            low = slice(a * LANES, (a + 1) * LANES)
            high = slice(half + a * LANES, half + (a + 1) * LANES)
            total = [0.0, 0.0, 0.0, 0.0]
            for slot in range(2):
                p_re, p_im = acc[slot, :beams, low], acc[slot, beams:, low]
                q_re, q_im = acc[slot, :beams, high], acc[slot, beams:, high]
                c, s = cos_t[slot, :, low], sin_t[slot, :, low]
                (rc, rs), first = turns[slot]
                qc, qs = first if a == 0 else (rc, rs)
                u_re, u_im = p_re * c - q_re * s, p_im * c - q_im * s
                v_re, v_im = q_re * c + p_re * s, q_im * c + p_im * s
                total[0] += u_re * rc - u_im * rs
                total[1] += u_im * rc + u_re * rs
                total[2] += v_re * qc - v_im * qs
                total[3] += v_im * qc + v_re * qs
            merged[:beams, low] = total[0].astype(BF16)
            merged[beams:, low] = total[1].astype(BF16)
            merged[:beams, high] = total[2].astype(BF16)
            merged[beams:, high] = total[3].astype(BF16)

        @pl.when(level == 0)
        def _():
            table_copies[1].wait()

        for j in order:
            cols = slice(j * CHUNK, (j + 1) * CHUNK)
            result = jnp.dot(merged[...], inv[:, cols], preferred_element_type=F32).astype(BF16)

            @pl.when(level < NUM_COMBINES - 1)
            def _():
                full[level + 1, j, 0, mine, :] = result[:beams]
                full[level + 1, j, 1, mine, :] = result[beams:]
                distribute(level + 1, j)

            @pl.when(level == NUM_COMBINES - 1)
            def _():
                out_ref[0, :, cols] = result[:beams]
                out_ref[1, :, cols] = result[beams:]

        return carry

    lax.fori_loop(0, NUM_COMBINES, level_body, 0)

    def drain(level, carry):
        w_copy(level).wait_send()
        for j in range(chunks):
            core_copy(level, j).wait_send()
            z_copy(level, j).wait_send()

        for slot in range(2):

            @pl.when(has_right)
            def _():
                edge_copy(level, slot, 0).wait_send()

            @pl.when(has_left)
            def _():
                edge_copy(level, slot, 1).wait_send()

        return carry

    lax.fori_loop(0, NUM_COMBINES, drain, 0)


def shards(pictures, floors, blends, bins, parts, rots):
    current = pictures[:, 0]
    _, beams, strip_len = current.shape
    length = strip_len + 2 * GUARD
    half = length // 2
    chunks = strip_len // CHUNK
    rows = 2 * beams
    forward, inverse = transform_tables(strip_len)
    n = NUM_COMBINES
    vmem = pl.BlockSpec(memory_space=pltpu.VMEM)
    dma = pltpu.SemaphoreType.DMA
    out = pl.pallas_call(
        functools.partial(kernel, lax.axis_size("aper"), lax.axis_size("strip")),
        out_shape=jax.ShapeDtypeStruct(current.shape, BF16),
        in_specs=[vmem] * 6 + [pl.BlockSpec(memory_space=pl.ANY)] * 2,
        out_specs=vmem,
        scratch_shapes=[
            pltpu.VMEM((length, length), BF16),
            pltpu.VMEM((length, strip_len), BF16),
            pltpu.VMEM((n, chunks, 2, 2 * beams, CHUNK), BF16),
            pltpu.VMEM((n, beams, 2 * beams), BF16),
            pltpu.VMEM((n, beams, 2 * beams), BF16),
            pltpu.VMEM((n, beams, 2 * beams), BF16),
            pltpu.VMEM((n, chunks, rows, CHUNK), BF16),
            pltpu.VMEM((n, chunks, rows, CHUNK), BF16),
            pltpu.VMEM((n, rows, 2 * GUARD), BF16),
            pltpu.VMEM((n, rows, length), BF16),
            pltpu.VMEM((2, rows, length), F32),
            pltpu.VMEM((rows, length), BF16),
            pltpu.VMEM((2, beams, half), F32),
            pltpu.VMEM((2, beams, half), F32),
            dma((2,)),
            dma((n, chunks)),
            dma((n, chunks)),
            dma((n, 2, 2)),
            dma((n, 2, 2)),
            dma((n, chunks)),
            dma((n, chunks)),
            dma((n,)),
            dma((n,)),
        ],
        compiler_params=pltpu.CompilerParams(
            collective_id=0, has_side_effects=True, vmem_limit_bytes=56 * 1024 * 1024
        ),
    )(
        current,
        floors[:, 0],
        blends[:, 0],
        bins[:, 0],
        parts[:, 0],
        rots[:, 0],
        jnp.asarray(forward),
        jnp.asarray(inverse),
    )
    return out[:, None]


def solution(mesh):
    tables = P(None, ("group", "aper"), None, "beam")
    pictures = P(None, ("group", "aper"), "beam", "strip")
    return jax.shard_map(
        shards,
        mesh=mesh,
        in_specs=(pictures,) + (tables,) * 5,
        out_specs=pictures,
        check_vma=False,
    )
```

```python
import functools
import math

import jax
import jax.numpy as jnp
import ml_dtypes
import numpy as np
from jax import lax
from jax.experimental import pallas as pl
from jax.experimental.pallas import tpu as pltpu
from jax.sharding import PartitionSpec as P

GUARD = 128
NUM_COMBINES = 4
CHUNK = 256
LANES = 128
MESH = pl.DeviceIdType.MESH
F32 = jnp.float32
BF16 = jnp.bfloat16


def transform_tables(strip_len):
    length = strip_len + 2 * GUARD
    half = length // 2
    sample = np.concatenate(
        [np.arange(GUARD, GUARD + strip_len), np.arange(GUARD), np.arange(GUARD + strip_len, length)]
    )
    freq = np.arange(half)
    angle = (sample[:, None] * freq[None, :] % length) * (2.0 * np.pi / length)
    cosines = np.cos(angle)
    sines = np.sin(angle)
    sines[:, 0] = 1.0 - 2.0 * (sample % 2)
    forward = np.concatenate([cosines, sines], axis=1).astype(ml_dtypes.bfloat16)
    inverse = forward[:strip_len].astype(np.float32).T.copy()
    inverse[0] *= 0.5
    inverse[half] *= 0.5
    return forward, inverse.astype(ml_dtypes.bfloat16)


def kernel(
    n_aper,
    n_strip,
    x_ref,
    floor_ref,
    blend_ref,
    bins_ref,
    part_ref,
    rot_ref,
    fwd_hbm,
    inv_hbm,
    out_ref,
    fwd,
    inv,
    full,
    w_own,
    w_send,
    w_recv,
    s_main,
    r_main,
    r_guard,
    x_own,
    acc,
    merged,
    cos_t,
    sin_t,
    table_sem,
    core_send,
    core_recv,
    edge_send,
    edge_recv,
    z_send,
    z_recv,
    w_send_sem,
    w_recv_sem,
):
    beams = x_ref.shape[1]
    all_beams = 2 * beams
    strip_len = x_ref.shape[2]
    chunks = strip_len // CHUNK
    length = strip_len + 2 * GUARD
    half = length // 2
    blocks = half // LANES
    bits = n_aper.bit_length() - 1
    order = [0, chunks - 1] + list(range(1, chunks - 1))

    aper = lax.axis_index("aper")
    strip = lax.axis_index("strip")
    beam = lax.axis_index("beam")
    other = 1 - beam
    has_left = strip > 0
    has_right = strip < n_strip - 1
    mine = pl.ds(pl.multiple_of(beam * beams, beams), beams)

    table_copies = [
        pltpu.make_async_copy(fwd_hbm, fwd, table_sem.at[0]),
        pltpu.make_async_copy(inv_hbm, inv, table_sem.at[1]),
    ]
    for copy in table_copies:
        copy.start()

    def flip(bit):
        return aper + bit - 2 * bit * ((aper // bit) % 2)

    def level_bit(level):
        bit = 1 << ((NUM_COMBINES - 1) % bits)
        for at in range(NUM_COMBINES - 1):
            bit = jnp.where(level == at, 1 << (at % bits), bit)
        return bit

    barrier = pltpu.get_barrier_semaphore()

    def greet(where):
        pl.semaphore_signal(barrier, inc=1, device_id=where, device_id_type=MESH)

    greet({"beam": other})
    partner_bits = sorted({1 << (at % bits) for at in range(NUM_COMBINES)})
    for bit in partner_bits:
        greet({"aper": flip(bit)})

    @pl.when(has_left)
    def _():
        greet({"strip": strip - 1})

    @pl.when(has_right)
    def _():
        greet({"strip": strip + 1})

    sides = has_left.astype(jnp.int32) + has_right.astype(jnp.int32)
    pl.semaphore_wait(barrier, 1 + len(partner_bits) + sides)

    def core_copy(level, j):
        place = full.at[level, j, :, mine, :]
        return pltpu.make_async_remote_copy(
            place, place, core_send.at[level, j], core_recv.at[level, j], {"beam": other}, MESH
        )

    def edge_copy(level, slot, side, outward=True):
        target = strip + 1 if (side == 0) == outward else strip - 1
        if slot == 0:
            at = strip_len - GUARD if side == 0 else 0
            source = x_own.at[level, :, pl.ds(at, GUARD)]
            place = x_own.at[level, :, pl.ds(strip_len + side * GUARD, GUARD)]
        else:
            j, at = (chunks - 1, CHUNK - GUARD) if side == 0 else (0, 0)
            source = r_main.at[level, j, :, pl.ds(at, GUARD)]
            place = r_guard.at[level, :, pl.ds(side * GUARD, GUARD)]
        return pltpu.make_async_remote_copy(
            source,
            place,
            edge_send.at[level, slot, side],
            edge_recv.at[level, slot, side],
            {"strip": target},
            MESH,
        )

    def send_edges(level, slot, j):
        if j == 0:

            @pl.when(has_left)
            def _():
                edge_copy(level, slot, 1).start()

        if j == chunks - 1:

            @pl.when(has_right)
            def _():
                edge_copy(level, slot, 0).start()

    def await_edges(level, slot):
        for side, there in ((0, has_left), (1, has_right)):

            @pl.when(there)
            def _():
                edge_copy(level, slot, side, outward=False).wait_recv()

    def z_copy(level, j):
        return pltpu.make_async_remote_copy(
            s_main.at[level, j],
            r_main.at[level, j],
            z_send.at[level, j],
            z_recv.at[level, j],
            {"aper": flip(level_bit(level))},
            MESH,
        )

    def w_copy(level):
        return pltpu.make_async_remote_copy(
            w_send.at[level],
            w_recv.at[level],
            w_send_sem.at[level],
            w_recv_sem.at[level],
            {"aper": flip(level_bit(level))},
            MESH,
        )

    def distribute(level, j):
        core_copy(level, j).start()

    for j in order:
        full[0, j, :, mine, :] = x_ref[:, :, j * CHUNK : (j + 1) * CHUNK]
        distribute(0, j)

    eye = lax.broadcasted_iota(jnp.int32, (beams, beams), 0) == lax.broadcasted_iota(
        jnp.int32, (beams, beams), 1
    )

    def column(ref, level, slot):
        row = ref[level, slot : slot + 1, :].astype(F32)
        return jnp.sum(jnp.where(eye, jnp.broadcast_to(row, (beams, beams)), 0.0), axis=1, keepdims=True)

    def weights_of(level, slot):
        source = lax.broadcasted_iota(jnp.int32, (beams, all_beams), 1).astype(F32)
        chosen = column(floor_ref, level, slot)
        fraction = column(blend_ref, level, slot)
        return (
            jnp.where(source == chosen, 1.0 - fraction, 0.0)
            + jnp.where(source == chosen + 1.0, fraction, 0.0)
        ).astype(BF16)

    def send_weights(level, carry):
        w_send[level] = weights_of(level, 1)
        w_copy(level).start()
        return carry

    lax.fori_loop(0, NUM_COMBINES, send_weights, 0)

    @pl.when(jnp.logical_not(has_left))
    def _():
        none = jnp.zeros((NUM_COMBINES, 2 * beams, GUARD), BF16)
        x_own[:, :, strip_len + 0 * GUARD : strip_len + 1 * GUARD] = none
        r_guard[:, :, 0 * GUARD : 1 * GUARD] = none

    @pl.when(jnp.logical_not(has_right))
    def _():
        none = jnp.zeros((NUM_COMBINES, 2 * beams, GUARD), BF16)
        x_own[:, :, strip_len + 1 * GUARD : strip_len + 2 * GUARD] = none
        r_guard[:, :, 1 * GUARD : 2 * GUARD] = none

    def own_weights(level, carry):
        w_own[level] = weights_of(level, 0)
        return carry

    lax.fori_loop(0, NUM_COMBINES, own_weights, 0)

    step = 2.0 * math.pi / length
    lane = lax.broadcasted_iota(jnp.int32, (beams, LANES), 1)

    def level_body(level, carry):
        w_copy(level).wait_recv()
        weights = jnp.concatenate([w_recv[level], w_own[level]], axis=0)
        for j in order:
            core_copy(level, j).wait_recv()
            for c in range(2):
                mixed = jnp.dot(weights, full[level, j, c], preferred_element_type=F32).astype(BF16)
                s_main[level, j, c * beams : (c + 1) * beams, :] = mixed[:beams]
                x_own[level, c * beams : (c + 1) * beams, j * CHUNK : (j + 1) * CHUNK] = mixed[beams:]
            z_copy(level, j).start()
            send_edges(level, 0, j)
        turns = []
        for slot in range(2):
            sigma = column(bins_ref, level, slot) + column(part_ref, level, slot)
            rot = column(rot_ref, level, slot)
            base = lane.astype(F32) * (step * sigma)
            base_cos, base_sin = jnp.cos(base), jnp.sin(base)
            lead = lane.astype(F32) * (step * LANES * sigma)
            lead_cos, lead_sin = jnp.cos(lead), jnp.sin(lead)
            for a in range(blocks):
                a_cos, a_sin = lead_cos[:, a : a + 1], lead_sin[:, a : a + 1]
                cos_t[slot, :, a * LANES : (a + 1) * LANES] = base_cos * a_cos - base_sin * a_sin
                sin_t[slot, :, a * LANES : (a + 1) * LANES] = base_sin * a_cos + base_cos * a_sin
            nyquist = rot + jnp.where(lane == 0, math.pi * sigma, 0.0)
            scale = 2.0 / length
            first = (jnp.cos(nyquist) * scale, jnp.sin(nyquist) * scale)
            rest = (first[0][:, 1:2], first[1][:, 1:2])
            turns.append((rest, first))

        @pl.when(level == 0)
        def _():
            table_copies[0].wait()

        for at in range(0, length, CHUNK):
            acc[0, :, at : at + CHUNK] = jnp.dot(
                x_own[level, :, :strip_len], fwd[:strip_len, at : at + CHUNK], preferred_element_type=F32
            )
        for i, j in enumerate(order + [chunks]):
            if j < chunks:
                z_copy(level, j).wait_recv()
                send_edges(level, 1, j)
                piece = r_main[level, j]
            else:
                await_edges(level, 1)
                piece = r_guard[level]
            if i == chunks - 1:
                await_edges(level, 0)
                own = x_own[level, :, strip_len:]
                for at in range(0, length, CHUNK):
                    acc[0, :, at : at + CHUNK] += jnp.dot(
                        own, fwd[strip_len:, at : at + CHUNK], preferred_element_type=F32
                    )
            for at in range(0, length, CHUNK):
                term = jnp.dot(piece, fwd[j * CHUNK : (j + 1) * CHUNK, at : at + CHUNK], preferred_element_type=F32)
                if i == 0:
                    acc[1, :, at : at + CHUNK] = term
                else:
                    acc[1, :, at : at + CHUNK] += term

        for a in range(blocks):
            low = slice(a * LANES, (a + 1) * LANES)
            high = slice(half + a * LANES, half + (a + 1) * LANES)
            total = [0.0, 0.0, 0.0, 0.0]
            for slot in range(2):
                p_re, p_im = acc[slot, :beams, low], acc[slot, beams:, low]
                q_re, q_im = acc[slot, :beams, high], acc[slot, beams:, high]
                c, s = cos_t[slot, :, low], sin_t[slot, :, low]
                (rc, rs), first = turns[slot]
                qc, qs = first if a == 0 else (rc, rs)
                u_re, u_im = p_re * c - q_re * s, p_im * c - q_im * s
                v_re, v_im = q_re * c + p_re * s, q_im * c + p_im * s
                total[0] += u_re * rc - u_im * rs
                total[1] += u_im * rc + u_re * rs
                total[2] += v_re * qc - v_im * qs
                total[3] += v_im * qc + v_re * qs
            merged[:beams, low] = total[0].astype(BF16)
            merged[beams:, low] = total[1].astype(BF16)
            merged[:beams, high] = total[2].astype(BF16)
            merged[beams:, high] = total[3].astype(BF16)

        @pl.when(level == 0)
        def _():
            table_copies[1].wait()

        for j in order:
            cols = slice(j * CHUNK, (j + 1) * CHUNK)
            result = jnp.dot(merged[...], inv[:, cols], preferred_element_type=F32).astype(BF16)

            @pl.when(level < NUM_COMBINES - 1)
            def _():
                full[level + 1, j, 0, mine, :] = result[:beams]
                full[level + 1, j, 1, mine, :] = result[beams:]
                distribute(level + 1, j)

            @pl.when(level == NUM_COMBINES - 1)
            def _():
                out_ref[0, :, cols] = result[:beams]
                out_ref[1, :, cols] = result[beams:]

        return carry

    lax.fori_loop(0, NUM_COMBINES, level_body, 0)

    def drain(level, carry):
        w_copy(level).wait_send()
        for j in range(chunks):
            core_copy(level, j).wait_send()
            z_copy(level, j).wait_send()

        for slot in range(2):

            @pl.when(has_right)
            def _():
                edge_copy(level, slot, 0).wait_send()

            @pl.when(has_left)
            def _():
                edge_copy(level, slot, 1).wait_send()

        return carry

    lax.fori_loop(0, NUM_COMBINES, drain, 0)


def shards(pictures, floors, blends, bins, parts, rots):
    current = pictures[:, 0]
    _, beams, strip_len = current.shape
    length = strip_len + 2 * GUARD
    half = length // 2
    chunks = strip_len // CHUNK
    rows = 2 * beams
    forward, inverse = transform_tables(strip_len)
    n = NUM_COMBINES
    vmem = pl.BlockSpec(memory_space=pltpu.VMEM)
    dma = pltpu.SemaphoreType.DMA
    out = pl.pallas_call(
        functools.partial(kernel, lax.axis_size("aper"), lax.axis_size("strip")),
        out_shape=jax.ShapeDtypeStruct(current.shape, BF16),
        in_specs=[vmem] * 6 + [pl.BlockSpec(memory_space=pl.ANY)] * 2,
        out_specs=vmem,
        scratch_shapes=[
            pltpu.VMEM((length, length), BF16),
            pltpu.VMEM((length, strip_len), BF16),
            pltpu.VMEM((n, chunks, 2, 2 * beams, CHUNK), BF16),
            pltpu.VMEM((n, beams, 2 * beams), BF16),
            pltpu.VMEM((n, beams, 2 * beams), BF16),
            pltpu.VMEM((n, beams, 2 * beams), BF16),
            pltpu.VMEM((n, chunks, rows, CHUNK), BF16),
            pltpu.VMEM((n, chunks, rows, CHUNK), BF16),
            pltpu.VMEM((n, rows, 2 * GUARD), BF16),
            pltpu.VMEM((n, rows, length), BF16),
            pltpu.VMEM((2, rows, length), F32),
            pltpu.VMEM((rows, length), BF16),
            pltpu.VMEM((2, beams, half), F32),
            pltpu.VMEM((2, beams, half), F32),
            dma((2,)),
            dma((n, chunks)),
            dma((n, chunks)),
            dma((n, 2, 2)),
            dma((n, 2, 2)),
            dma((n, chunks)),
            dma((n, chunks)),
            dma((n,)),
            dma((n,)),
        ],
        compiler_params=pltpu.CompilerParams(
            collective_id=0, has_side_effects=True, vmem_limit_bytes=56 * 1024 * 1024
        ),
    )(
        current,
        floors[:, 0],
        blends[:, 0],
        bins[:, 0],
        parts[:, 0],
        rots[:, 0],
        jnp.asarray(forward),
        jnp.asarray(inverse),
    )
    return out[:, None]


def solution(mesh):
    tables = P(None, ("group", "aper"), None, "beam")
    pictures = P(None, ("group", "aper"), "beam", "strip")
    return jax.shard_map(
        shards,
        mesh=mesh,
        in_specs=(pictures,) + (tables,) * 5,
        out_specs=pictures,
        check_vma=False,
    )
```
